32 devices in a mesh: groups: 2 (over y), expert: 16 (over z, x, core).
Axes of the slice: x: 2, y: 2, z: 4, core: 2. Of those that a mesh axis runs over, the one named last changes fastest.
Arguments:
- tokens: bfloat16 [2048, 2048], P(('groups', 'expert')), parts along dimension 0, may hold values from -6 to 6
- scales: bfloat16 [2048, 16], P(('groups', 'expert')), parts along dimension 0, may hold values from 0.29882812 to 3
- expert_ids: int32 [2048, 8], P(('groups', 'expert')), parts along dimension 0, may hold values from 0 to 15, all different within a row; in each aligned block of 64 rows (0 to 63, 64 to 127, ...) at most 64 rows name the same one
- gate_weights: float32 [2048, 8], P(('groups', 'expert')), parts along dimension 0, may hold values from 0.02 to 0.3
- w_gate: bfloat16 [16, 2048, 768], P('expert'), may hold values from -0.125 to 0.125
- w_up: bfloat16 [16, 2048, 768], P('expert'), may hold values from -0.125 to 0.125
- w_down: bfloat16 [16, 768, 2048], P('expert'), may hold values from -0.21875 to 0.21875
Outputs:
- combined: bfloat16 [2048, 2048], P(('groups', 'expert')), parts along dimension 0
The draws below stay inside these ranges and needn't reach their ends.
There are 2 independent parts, one for each index of `groups`. The reference program is written for one: setup_inputs(seed, part) draws one part's arguments, and reference() takes and returns one part's arrays. A program takes and returns all parts, laid end to end along the dimension named above; an argument that names none is the same for every part. Nothing has to cross between parts.
Inputs may be any that keep to these rules, and one draw needn't show every extreme that they name: `expert_ids`: each token names 8 different experts. Among the 64 tokens of one index of expert (aligned blocks of rows) no expert is named by more than 64 tokens, and in some blocks some expert is named by exactly 64.
All inputs are finite; a program needn't handle non-finite values.
Results may differ from the reference program's by a relative error of at most 0.0071.
Values may be sent and summed in bfloat16 or wider, within the bound.
No kernel may reach another device: no remote copies, remote signals or barrier semaphores. Data moves between devices by JAX's collectives and lax.ppermute only.
A program may use at most 128 MiB of HBM per device.

```python
import math
import jax
import jax.numpy as jnp
import numpy as np
from jax import lax

D = 2048
FF = 768
TOP = 8
TOK_DEV = 64
EXPERTS = 16
TOKENS = 1024
CAP = 64
N_EXPERT = 16


def steps_of(key, extent, split, smallest, high):
    def one(dim, blocks):
        draws = jax.random.uniform(jax.random.fold_in(jax.random.fold_in(key, 6), dim), (blocks,), jnp.float32, smallest / len(split), high / len(split))
        return jnp.repeat(jnp.exp(draws), extent[dim] // blocks).reshape((-1,) + (1,) * (len(extent) - dim - 1))

    level = one(*split[0])
    for cut in split[1:]:
        level = level * one(*cut)
    return level


def shared_out(key, own, number, rows, amount, top, reach, skew):
    ranking = jax.random.permutation(key, amount)
    packed, common = load_shares(amount, rows * top, reach, skew, True), load_shares(amount, rows * top, reach, skew, False)
    places = jnp.arange(amount)

    def named(sizes, offset_by):
        used = int((sizes > 0).sum())
        fixed = max(1, used // 4)
        passed = fixed + (places - fixed + offset_by * (used - fixed)) % max(1, amount - fixed)
        return jnp.zeros((amount,), jnp.int32).at[ranking[jnp.where(places < fixed, places, passed)]].set(jnp.asarray(sizes, jnp.int32))

    sizes = jnp.where(number % 4 == 0, named(packed, number // 4), named(common, number - number // 4 - 1))
    mixed = jax.random.permutation(jax.random.fold_in(own, 3), amount)
    donor, taker = mixed[0:amount // 2 * 2:2], mixed[1:amount // 2 * 2:2]
    margin = jnp.minimum(sizes[donor] - 1, reach - sizes[taker]) // 2
    margin = jnp.where((donor == ranking[0]) | (taker == ranking[0]) | (sizes[taker] == 0), 0, jnp.maximum(margin, 0))
    passed = jax.random.randint(jax.random.fold_in(own, 4), (amount // 2,), 0, 1 << 20) % (margin + 1)
    sizes = sizes.at[donor].add(-passed).at[taker].add(passed)
    labels = jnp.searchsorted(jnp.cumsum(sizes), jnp.arange(rows * top), side="right").astype(jnp.int32)
    grid = labels.reshape(top, rows).T
    grid = grid[jax.random.permutation(jax.random.fold_in(own, 1), rows)]
    offset_by = jax.random.randint(jax.random.fold_in(own, 2), (rows, 1), 0, top)
    return jnp.take_along_axis(grid, (jnp.arange(top)[None, :] + offset_by) % top, axis=1)


def load_shares(amount, total, most, skew, full):
    loads = [(1 << 20) // math.isqrt(grade ** skew) + 1 for grade in range(1, amount + 1)]
    largest = most if full else min(most, max(-(-total // amount), total * loads[0] // sum(loads)))
    least = 1 if total - largest >= amount - 1 else 0
    holding, surplus = [largest] + [least] * (amount - 1), total - largest - least * (amount - 1)
    while surplus > 0:
        free = [i for i in range(1, amount) if holding[i] < largest] or [i for i in range(1, amount) if holding[i] < most]
        whole, budget = sum([loads[i] for i in free]), surplus
        for i in free:
            more = min(most - holding[i], max(1, budget * loads[i] // whole), surplus)
            holding[i] = holding[i] + more
            surplus = surplus - more
    return np.array(holding)


def normal_values(key, shape, scale, reach, split=(), kind=jnp.bfloat16):
    values = jax.random.normal(key, shape, jnp.float32) * scale
    if len(split) > 0:
        values = steps_of(key, shape, split, -0.22, 0.18) * values
    return jnp.clip(values, min=-reach, max=reach).astype(kind)


def setup_inputs(seed: int = 0, part: int = 0) -> dict:
    key_of = jax.random.split(jax.random.key(seed), 8)
    part_splits = jax.random.split(jax.random.fold_in(key_of[7], part), 8)
    tokens = normal_values(part_splits[0], (TOKENS, D), 1.0, 6.0, ((0, 16),))
    scales = jnp.clip(jnp.exp(math.log(3.0) - 2.306499 * jax.random.uniform(part_splits[1], (TOKENS, D // 128), jnp.float32) ** steps_of(part_splits[1], (TOKENS, D // 128), ((0, 16),), -0.2, 0.2)), 0.29882812, 3.0).astype(jnp.bfloat16)
    expert_ids_keys = jax.random.split(jax.random.fold_in(part_splits[2], 1), TOKENS // TOK_DEV)
    expert_ids_turns = jax.random.permutation(jax.random.fold_in(part_splits[2], 3), TOKENS // TOK_DEV)
    expert_ids = jax.vmap(lambda own, number: shared_out(jax.random.fold_in(part_splits[2], 2), own, number, TOK_DEV, EXPERTS, TOP, CAP, 2))(expert_ids_keys, expert_ids_turns).reshape((TOKENS, TOP))
    gate_weights = jnp.clip(0.02 + 0.28 * jax.random.uniform(part_splits[3], (TOKENS, TOP), jnp.float32) ** steps_of(part_splits[3], (TOKENS, TOP), ((0, 16),), -0.2, 0.2), 0.02, 0.3)
    w_gate = normal_values(key_of[4], (EXPERTS, D, FF), D ** -0.5, 0.125, ((0, 16),))
    w_up = normal_values(key_of[5], (EXPERTS, D, FF), D ** -0.5, 0.125, ((0, 16),))
    w_down = normal_values(key_of[6], (EXPERTS, FF, D), FF ** -0.5, 0.21875, ((0, 16),))
    return {"tokens": tokens, "scales": scales, "expert_ids": expert_ids, "gate_weights": gate_weights, "w_gate": w_gate, "w_up": w_up, "w_down": w_down}


def dequantize(values, scales):
    row_count, feature_width = values.shape
    blocks = scales.shape[1]
    scaled = values.astype(jnp.float32).reshape(row_count, blocks, feature_width // blocks) * scales.astype(jnp.float32)[:, :, None]
    return scaled.reshape(row_count, feature_width).astype(jnp.bfloat16)


def expert_block(inputs, gate_matrix, up_matrix, down_matrix):
    gate_part = jnp.dot(inputs, gate_matrix, preferred_element_type=jnp.float32)
    up_part = jnp.dot(inputs, up_matrix, preferred_element_type=jnp.float32)
    hidden = (jax.nn.silu(gate_part) * up_part).astype(jnp.bfloat16)
    return jnp.dot(hidden, down_matrix, preferred_element_type=jnp.float32).astype(jnp.bfloat16)


def reference(tokens, scales, expert_ids, gate_weights, w_gate, w_up, w_down):
    pair_count = TOKENS * TOP
    slot_count = N_EXPERT * CAP
    activations = dequantize(tokens, scales)
    padded_rows = jnp.concatenate([activations, jnp.zeros((1, D), jnp.bfloat16)], axis=0)
    flat_ids = expert_ids.reshape(-1).astype(jnp.int32)
    onehot = (flat_ids[:, None] == jnp.arange(EXPERTS, dtype=jnp.int32)[None, :]).astype(jnp.int32)
    position = jnp.sum((jnp.cumsum(onehot, axis=0) - onehot) * onehot, axis=1).astype(jnp.int32)
    table = jnp.full((EXPERTS, slot_count), pair_count, jnp.int32)
    table = table.at[flat_ids, position].set(jnp.arange(pair_count, dtype=jnp.int32))
    flat_weights = jnp.concatenate([gate_weights.reshape(-1), jnp.zeros((1,), jnp.float32)])

    def visit(running, expert):
        pairs = table[expert]
        token_index = pairs // TOP
        outputs = expert_block(padded_rows[token_index], w_gate[expert], w_up[expert], w_down[expert])
        weighted = flat_weights[pairs][:, None] * outputs.astype(jnp.float32)
        return running.at[token_index].add(weighted), None

    running, ignored = lax.scan(visit, jnp.zeros((TOKENS + 1, D), jnp.float32), jnp.arange(EXPERTS, dtype=jnp.int32))
    return running[:TOKENS].astype(jnp.bfloat16)
```

```python
import functools

import jax
import jax.numpy as jnp
from jax import lax
from jax.experimental import pallas as pl
from jax.experimental.pallas import tpu as pltpu
from jax.sharding import PartitionSpec as P

LANES = 128


def dequantize(values, scales):
    array_shape = values.shape
    blocks = scales.shape[-1]
    split_shape = array_shape[:-1] + (blocks, array_shape[-1] // blocks)
    scaled = values.astype(jnp.float32).reshape(split_shape) * scales.astype(jnp.float32)[..., None]
    return scaled.reshape(array_shape).astype(jnp.bfloat16)


def apply_experts(values, scale_rows, w_gate, w_up, w_down):
    inputs = dequantize(values, scale_rows)
    gate_part = jnp.einsum("pecd,edf->pecf", inputs, w_gate, preferred_element_type=jnp.float32)
    up_part = jnp.einsum("pecd,edf->pecf", inputs, w_up, preferred_element_type=jnp.float32)
    hidden = (jax.nn.silu(gate_part) * up_part).astype(jnp.bfloat16)
    return jnp.einsum("pecf,efd->pecd", hidden, w_down, preferred_element_type=jnp.float32).astype(
        jnp.bfloat16
    )


def routed(tokens, scales, expert_ids, gate_weights, w_gate, w_up, w_down):
    peer_count = lax.axis_size("expert")
    token_count, feature_width = tokens.shape
    top_count = expert_ids.shape[1]
    local_experts = w_gate.shape[0]
    expert_total = peer_count * local_experts
    capacity = 2 * token_count * top_count // expert_total
    blocks = scales.shape[1]
    flat_ids = expert_ids.reshape(-1)
    onehot = (flat_ids[:, None] == jnp.arange(expert_total, dtype=jnp.int32)[None, :]).astype(
        jnp.int32
    )
    position = jnp.sum((jnp.cumsum(onehot, axis=0) - onehot) * onehot, axis=1)
    slot_index = flat_ids * capacity + position
    source_token = jnp.arange(token_count * top_count, dtype=jnp.int32) // top_count
    send_values = (
        jnp.zeros((expert_total * capacity, feature_width), jnp.bfloat16)
        .at[slot_index]
        .set(tokens[source_token])
    )
    send_values = send_values.reshape(peer_count, local_experts, capacity, feature_width)
    send_scales = (
        jnp.zeros((expert_total * capacity, blocks), jnp.bfloat16)
        .at[slot_index]
        .set(scales[source_token])
    )
    send_scales = send_scales.reshape(peer_count, local_experts, capacity, blocks)
    outputs = apply_experts(
        lax.all_to_all(send_values, "expert", split_axis=0, concat_axis=0, tiled=True),
        lax.all_to_all(send_scales, "expert", split_axis=0, concat_axis=0, tiled=True),
        w_gate,
        w_up,
        w_down,
    )
    returned = lax.all_to_all(outputs, "expert", split_axis=0, concat_axis=0, tiled=True)
    gathered = returned.reshape(expert_total * capacity, feature_width)[slot_index]
    gathered = gathered.reshape(token_count, top_count, feature_width)
    combined = jnp.sum(gate_weights[:, :, None] * gathered.astype(jnp.float32), axis=1)
    return combined.astype(jnp.bfloat16)


def pack_rows(tokens, scales, expert_ids, gate_weights, expert_total):
    activations = dequantize(tokens, scales)
    chosen = expert_ids[:, :, None] == jnp.arange(expert_total, dtype=jnp.int32)[None, None, :]
    dense = jnp.sum(jnp.where(chosen, gate_weights[:, :, None], 0.0), axis=1)
    terms = []
    for _ in range(3):
        term = dense.astype(jnp.bfloat16)
        dense = dense - term.astype(jnp.float32)
        terms.append(term)
    spare = -3 * expert_total % LANES
    terms.append(jnp.zeros((tokens.shape[0], spare), jnp.bfloat16))
    return jnp.concatenate([activations] + terms, axis=1)


def expert_kernel(expert_total, me_ref, a0, a1, a2, a3, gate_ref, up_ref, down_ref, q0, q1, q2, q3, rows, total):
    step = pl.program_id(0)
    blocks = (a0, a1, a2, a3)
    count = a0.shape[0]
    width = down_ref.shape[2]

    @pl.when(step == 0)
    def _():
        for index, block in enumerate(blocks):
            rows[index * count : (index + 1) * count, :] = block[:, :width]

    inputs = rows[...]
    gate_part = jnp.dot(inputs, gate_ref[0], preferred_element_type=jnp.float32)
    up_part = jnp.dot(inputs, up_ref[0], preferred_element_type=jnp.float32)
    hidden = (gate_part / (1.0 + jnp.exp(-gate_part)) * up_part).astype(jnp.bfloat16)
    product = jnp.dot(hidden, down_ref[0], preferred_element_type=jnp.float32)

    @pl.when(step == 0)
    def _():
        total[...] = product

    @pl.when(step > 0)
    def _():
        total[...] += product

    @pl.when(step == pl.num_programs(0) - 1)
    def _():
        for index, (block, out) in enumerate(zip(blocks, (q0, q1, q2, q3), strict=True)):
            terms = block[:, width:].astype(jnp.float32)
            lane = lax.broadcasted_iota(jnp.int32, terms.shape, 1) % expert_total
            weight = jnp.sum(jnp.where(lane == me_ref[0], terms, 0.0), axis=1, keepdims=True)
            result = total[index * count : (index + 1) * count, :].astype(jnp.bfloat16)
            out[...] = (weight * result.astype(jnp.float32)).astype(out.dtype)


def weighted_outputs(expert_total, me, blocks, w_gate, w_up, w_down):
    count, packed = blocks[0].shape
    hidden_width, width = w_down.shape[1:]
    chunk = 256
    whole = pl.BlockSpec((count, packed), lambda s: (0, 0))
    out = pl.BlockSpec((count, width), lambda s: (0, 0))
    rows = 4 * count
    return pl.pallas_call(
        functools.partial(expert_kernel, expert_total),
        grid=(hidden_width // chunk,),
        in_specs=[pl.BlockSpec(memory_space=pltpu.SMEM)]
        + [whole] * 4
        + [pl.BlockSpec((1, width, chunk), lambda s: (0, 0, s))] * 2
        + [pl.BlockSpec((1, chunk, width), lambda s: (0, s, 0))],
        out_specs=[out] * 4,
        out_shape=[
            jax.ShapeDtypeStruct((count, width), jnp.bfloat16 if index % 2 else jnp.float32)
            for index in range(4)
        ],
        scratch_shapes=[pltpu.VMEM((rows, width), jnp.bfloat16), pltpu.VMEM((rows, width), jnp.float32)],
        compiler_params=pltpu.CompilerParams(vmem_limit_bytes=32 * 2**20),
        cost_estimate=pl.CostEstimate(
            flops=6 * rows * width * hidden_width,
            bytes_accessed=6 * width * hidden_width + 10 * rows * width,
            transcendentals=rows * hidden_width,
        ),
    )(me, *blocks, w_gate, w_up, w_down)


def gathered(tokens, scales, expert_ids, gate_weights, w_gate, w_up, w_down):
    peer_count = lax.axis_size("expert")

    def exchange(array, mask):
        return lax.ppermute(array, "expert", [(i, i ^ mask) for i in range(peer_count)])

    me = lax.axis_index("expert").astype(jnp.int32).reshape(1)
    columns = range(0, peer_count, 4)
    rows = {0: pack_rows(tokens, scales, expert_ids, gate_weights, peer_count)}
    for z in columns[1:]:
        rows[z] = exchange(rows[0], z)
    for z in columns:
        rows[z + 2] = exchange(rows[z], 2)
    for z in columns:
        for x in (z, z + 2):
            rows[x + 1] = exchange(rows[x], 1)
    sums = {}
    for z in columns:
        parts = weighted_outputs(peer_count, me, [rows[z + j] for j in range(4)], w_gate, w_up, w_down)
        own = parts[0] + exchange(parts[1], 1).astype(jnp.float32)
        other = parts[2] + exchange(parts[3], 1).astype(jnp.float32)
        sums[z] = own + exchange(other.astype(jnp.bfloat16), 2).astype(jnp.float32)
    combined = sums[0]
    for z in columns[1:]:
        combined = combined + exchange(sums[z].astype(jnp.bfloat16), z).astype(jnp.float32)
    return combined.astype(jnp.bfloat16)


def on_device(tokens, scales, expert_ids, gate_weights, w_gate, w_up, w_down):
    peer_count = lax.axis_size("expert")
    local_experts = w_gate.shape[0]
    capacity = 2 * tokens.shape[0] * expert_ids.shape[1] // (peer_count * local_experts)
    power_of_two = peer_count & (peer_count - 1) == 0
    whole = capacity >= tokens.shape[0] and local_experts == 1 and peer_count >= 4 and power_of_two
    layer = gathered if whole else routed
    return layer(tokens, scales, expert_ids, gate_weights, w_gate, w_up, w_down)


def solution(mesh):
    return jax.shard_map(
        on_device,
        mesh=mesh,
        in_specs=(
            P(("groups", "expert"), None),
            P(("groups", "expert"), None),
            P(("groups", "expert"), None),
            P(("groups", "expert"), None),
            P("expert", None, None),
            P("expert", None, None),
            P("expert", None, None),
        ),
        out_specs=P(("groups", "expert"), None),
        check_vma=False,
    )
```

```python
import functools

import jax
import jax.numpy as jnp
from jax import lax
from jax.experimental import pallas as pl
from jax.experimental.pallas import tpu as pltpu
from jax.sharding import PartitionSpec as P

LANES = 128
CHUNK = 256
STEPS = [
    ('A4', []),
    ('A8', []),
    ('A2', []),
    ('A1', []),
    ('A3', []),
    ('A12', []),
    ('A6', []),
    ('A5', []),
    ('A7', []),
    ('A10', []),
    ('A9', []),
    ('A11', []),
    ('A14', []),
    ('A13', []),
    ('A15', []),
    ('K0', []),
    ('O0', []),
    ('X0', []),
    ('K4', []),
    ('O4', []),
    ('X4', []),
    ('K8', []),
    ('O8', []),
    ('X8', []),
    ('K12', []),
    ('O12', []),
    ('X12', []),
    ('Z4', []),
    ('Z8', []),
    ('Z12', []),
]
VMEM_LIMIT = 24 * 2**20


def dequantize(values, scales):
    array_shape = values.shape
    blocks = scales.shape[-1]
    split_shape = array_shape[:-1] + (blocks, array_shape[-1] // blocks)
    scaled = values.astype(jnp.float32).reshape(split_shape) * scales.astype(jnp.float32)[..., None]
    return scaled.reshape(array_shape).astype(jnp.bfloat16)


def apply_experts(values, scale_rows, w_gate, w_up, w_down):
    inputs = dequantize(values, scale_rows)
    gate_part = jnp.einsum("pecd,edf->pecf", inputs, w_gate, preferred_element_type=jnp.float32)
    up_part = jnp.einsum("pecd,edf->pecf", inputs, w_up, preferred_element_type=jnp.float32)
    hidden = (jax.nn.silu(gate_part) * up_part).astype(jnp.bfloat16)
    return jnp.einsum("pecf,efd->pecd", hidden, w_down, preferred_element_type=jnp.float32).astype(
        jnp.bfloat16
    )


def routed(tokens, scales, expert_ids, gate_weights, w_gate, w_up, w_down):
    peer_count = lax.axis_size("expert")
    token_count, feature_width = tokens.shape
    top_count = expert_ids.shape[1]
    local_experts = w_gate.shape[0]
    expert_total = peer_count * local_experts
    capacity = 2 * token_count * top_count // expert_total
    blocks = scales.shape[1]
    flat_ids = expert_ids.reshape(-1)
    onehot = (flat_ids[:, None] == jnp.arange(expert_total, dtype=jnp.int32)[None, :]).astype(
        jnp.int32
    )
    position = jnp.sum((jnp.cumsum(onehot, axis=0) - onehot) * onehot, axis=1)
    slot_index = flat_ids * capacity + position
    source_token = jnp.arange(token_count * top_count, dtype=jnp.int32) // top_count
    send_values = (
        jnp.zeros((expert_total * capacity, feature_width), jnp.bfloat16)
        .at[slot_index]
        .set(tokens[source_token])
    )
    send_values = send_values.reshape(peer_count, local_experts, capacity, feature_width)
    send_scales = (
        jnp.zeros((expert_total * capacity, blocks), jnp.bfloat16)
        .at[slot_index]
        .set(scales[source_token])
    )
    send_scales = send_scales.reshape(peer_count, local_experts, capacity, blocks)
    outputs = apply_experts(
        lax.all_to_all(send_values, "expert", split_axis=0, concat_axis=0, tiled=True),
        lax.all_to_all(send_scales, "expert", split_axis=0, concat_axis=0, tiled=True),
        w_gate,
        w_up,
        w_down,
    )
    returned = lax.all_to_all(outputs, "expert", split_axis=0, concat_axis=0, tiled=True)
    gathered = returned.reshape(expert_total * capacity, feature_width)[slot_index]
    gathered = gathered.reshape(token_count, top_count, feature_width)
    combined = jnp.sum(gate_weights[:, :, None] * gathered.astype(jnp.float32), axis=1)
    return combined.astype(jnp.bfloat16)


def pack_kernel(expert_total, *refs):
    sources, out_ref, targets, sems = refs[:4], refs[4], refs[5:9], refs[9]
    tokens_ref, scales_ref, ids_ref, weights_ref = targets
    copies = [
        pltpu.make_async_copy(source, target, sems.at[index])
        for index, (source, target) in enumerate(zip(sources, targets, strict=True))
    ]
    for copy in copies:
        copy.start()
    count, width = tokens_ref.shape
    blocks = scales_ref.shape[0]
    size = width // blocks
    packed = out_ref.shape[1]
    square = (count, count)
    same = lax.broadcasted_iota(jnp.int32, square, 0) == lax.broadcasted_iota(jnp.int32, square, 1)
    same = same.astype(jnp.float32).astype(jnp.bfloat16)

    def turn(values):
        return lax.dot_general(
            same, values, (((1,), (1,)), ((), ())), preferred_element_type=jnp.float32
        )

    for copy in copies[1:]:
        copy.wait()
    line = lax.broadcasted_iota(jnp.int32, (packed - width, count), 0)
    dense = jnp.zeros(line.shape, jnp.float32)
    for k in range(ids_ref.shape[0]):
        dense += jnp.where(line % expert_total == ids_ref[k : k + 1, :], weights_ref[k : k + 1, :], 0.0)
    terms = jnp.zeros(line.shape, jnp.float32)
    for index in range(3):
        term = dense.astype(jnp.bfloat16).astype(jnp.float32)
        terms = jnp.where(line // expert_total == index, term, terms)
        dense = dense - term
    out_ref[:, width:] = turn(terms.astype(jnp.bfloat16)).astype(jnp.bfloat16)
    scales = turn(scales_ref[...])
    copies[0].wait()
    for block in range(blocks):
        columns = slice(block * size, (block + 1) * size)
        values = tokens_ref[:, columns].astype(jnp.float32) * scales[:, block : block + 1]
        out_ref[:, columns] = values.astype(jnp.bfloat16)


def pack_rows(tokens, scales, expert_ids, gate_weights, expert_total):
    count, width = tokens.shape
    packed = width + -(-3 * expert_total // LANES) * LANES
    arrays = (tokens, scales.T, expert_ids.T, gate_weights.T)
    return pl.pallas_call(
        functools.partial(pack_kernel, expert_total),
        in_specs=[pl.BlockSpec(memory_space=pl.ANY)] * 4,
        out_specs=pl.BlockSpec(memory_space=pltpu.VMEM),
        out_shape=jax.ShapeDtypeStruct((count, packed), jnp.bfloat16),
        scratch_shapes=[pltpu.VMEM(array.shape, array.dtype) for array in arrays]
        + [pltpu.SemaphoreType.DMA((4,))],
        compiler_params=pltpu.CompilerParams(vmem_limit_bytes=64 * 2**20),
        cost_estimate=pl.CostEstimate(flops=1, bytes_accessed=1, transcendentals=0),
    )(*arrays)


def experts_on(expert_total, me_ref, blocks, outs, gate_ref, up_ref, down_ref, hidden_ref):
    hidden_width, width = down_ref.shape[1:]
    inputs = jnp.concatenate([block[:, :width] for block in blocks], axis=0)
    for index in range(hidden_width // CHUNK):
        columns = slice(index * CHUNK, (index + 1) * CHUNK)
        gate_part = jnp.dot(inputs, gate_ref[0, :, columns], preferred_element_type=jnp.float32)
        up_part = jnp.dot(inputs, up_ref[0, :, columns], preferred_element_type=jnp.float32)
        hidden = gate_part / (1.0 + jnp.exp(-gate_part)) * up_part
        hidden_ref[:, columns] = hidden.astype(jnp.bfloat16)
    factors = []
    for block in blocks:
        terms = block[:, width:].astype(jnp.float32)
        lane = lax.broadcasted_iota(jnp.int32, terms.shape, 1) % expert_total
        factors.append(jnp.sum(jnp.where(lane == me_ref[0], terms, 0.0), axis=1, keepdims=True))
    factor = jnp.concatenate(factors, axis=0)
    hidden = hidden_ref[...]
    for start in range(0, width, 512):
        columns = slice(start, start + 512)
        result = jnp.dot(hidden, down_ref[0, :, columns], preferred_element_type=jnp.float32)
        result = factor * result.astype(jnp.bfloat16).astype(jnp.float32)
        row = 0
        for out in outs:
            out[:, columns] = result[row : row + out.shape[0], :].astype(out.dtype)
            row += out.shape[0]


def expert_kernel(expert_total, number, *refs):
    me_ref, blocks, weights, outs, hidden_ref = refs[0], refs[1 : 1 + number], refs[1 + number : 4 + number], refs[-4:-1], refs[-1]
    experts_on(expert_total, me_ref, blocks, outs, *weights, hidden_ref)


def weighted_outputs(expert_total, me, blocks, weights):
    count = blocks[0].shape[0]
    rows = sum(block.shape[0] for block in blocks)
    hidden_width, width = weights[2].shape[1:]
    vmem = pl.BlockSpec(memory_space=pltpu.VMEM)
    return pl.pallas_call(
        functools.partial(expert_kernel, expert_total, len(blocks)),
        in_specs=[pl.BlockSpec(memory_space=pltpu.SMEM)] + [vmem] * (len(blocks) + 3),
        out_specs=[vmem] * 3,
        out_shape=[
            jax.ShapeDtypeStruct((count, width), jnp.float32),
            jax.ShapeDtypeStruct((count, width), jnp.float32),
            jax.ShapeDtypeStruct((rows - 2 * count, width), jnp.bfloat16),
        ],
        scratch_shapes=[pltpu.VMEM((rows, hidden_width), jnp.bfloat16)],
        compiler_params=pltpu.CompilerParams(vmem_limit_bytes=VMEM_LIMIT),
        cost_estimate=pl.CostEstimate(flops=1, bytes_accessed=1, transcendentals=0),
    )(me, *blocks, *weights)


def gathered(tokens, scales, expert_ids, gate_weights, w_gate, w_up, w_down):
    peer_count = lax.axis_size("expert")

    def exchange(array, mask):
        return lax.ppermute(array, "expert", [(i, i ^ mask) for i in range(peer_count)])

    def after(array, names):
        if not names:
            return array
        return lax.optimization_barrier((array,) + tuple(done[name] for name in names))[0]

    me = lax.axis_index("expert").astype(jnp.int32).reshape(1)
    weights = (w_gate, w_up, w_down)
    done = {"A0": pack_rows(tokens, scales, expert_ids, gate_weights, peer_count)}
    own, other, sums = {}, {}, {}
    for step, ties in STEPS:
        kind, number = step[0], int(step[1:])
        if kind == "A":
            bit = number & -number if number % 4 else 1 << (number.bit_length() - 1)
            done[step] = exchange(after(done["A%d" % (number - bit)], ties), bit)
        elif kind == "B":
            pair = jnp.concatenate([done["A%d" % number], done["A%d" % (number + 2)]], axis=0)
            done[step] = exchange(after(pair, ties), 1)
        elif kind == "K":
            names = ["A%d" % number, "A%d" % (number + 2)]
            names += ["B%d" % number] if "B%d" % number in done else ["A%d" % (number + 1), "A%d" % (number + 3)]
            blocks = [done[name] for name in names]
            blocks[0] = after(blocks[0], ties)
            parts = weighted_outputs(peer_count, me, blocks, weights)
            done[step] = parts[0]
            own[number], other[number] = parts[:2], parts[2]
        elif kind == "O":
            got = exchange(other[number], 1).astype(jnp.float32)
            count = got.shape[0] // 2
            done[step] = (own[number][1] + got[count:]).astype(jnp.bfloat16)
            own[number] = own[number][0] + got[:count]
        elif kind == "X":
            done[step] = exchange(after(done["O%d" % number], ties), 2)
            sums[number] = own[number] + done[step].astype(jnp.float32)
        elif kind == "Z":
            done[step] = exchange(after(sums[number].astype(jnp.bfloat16), ties), number)
    combined = sums[0]
    for z in range(4, peer_count, 4):
        combined = combined + done["Z%d" % z].astype(jnp.float32)
    return combined.astype(jnp.bfloat16)


def on_device(tokens, scales, expert_ids, gate_weights, w_gate, w_up, w_down):
    peer_count = lax.axis_size("expert")
    local_experts = w_gate.shape[0]
    capacity = 2 * tokens.shape[0] * expert_ids.shape[1] // (peer_count * local_experts)
    power_of_two = peer_count & (peer_count - 1) == 0
    whole = capacity >= tokens.shape[0] and local_experts == 1 and peer_count >= 4 and power_of_two
    layer = gathered if whole else routed
    return layer(tokens, scales, expert_ids, gate_weights, w_gate, w_up, w_down)


def solution(mesh):
    return jax.shard_map(
        on_device,
        mesh=mesh,
        in_specs=(
            P(("groups", "expert"), None),
            P(("groups", "expert"), None),
            P(("groups", "expert"), None),
            P(("groups", "expert"), None),
            P("expert", None, None),
            P("expert", None, None),
            P("expert", None, None),
        ),
        out_specs=P(("groups", "expert"), None),
        check_vma=False,
    )
```

```python
import functools

import jax
import jax.numpy as jnp
from jax import lax
from jax.experimental import pallas as pl
from jax.experimental.pallas import tpu as pltpu
from jax.sharding import PartitionSpec as P

LANES = 128
CHUNK = 256
FIRST = 'K0'
FIRST_LIMIT = 41 * 2**20
STEPS = [
    ('A4', []),
    ('A8', []),
    ('A2', []),
    ('A1', []),
    ('A3', []),
    ('A12', []),
    ('A6', []),
    ('A5', []),
    ('A7', []),
    ('A10', []),
    ('A9', []),
    ('A11', []),
    ('A14', []),
    ('A13', []),
    ('A15', []),
    ('K0', []),
    ('K8', ['K0']),
    ('O8', []),
    ('X8', []),
    ('K4', ['K0']),
    ('O0', []),
    ('O4', []),
    ('X4', ['X8']),
    ('K12', ['O8']),
    ('O12', []),
    ('X12', []),
    ('X0', ['X12']),
    ('Z8', []),
    ('Z12', []),
    ('Z4', []),
]
VMEM_LIMIT = 24 * 2**20


def dequantize(values, scales):
    array_shape = values.shape
    blocks = scales.shape[-1]
    split_shape = array_shape[:-1] + (blocks, array_shape[-1] // blocks)
    scaled = values.astype(jnp.float32).reshape(split_shape) * scales.astype(jnp.float32)[..., None]
    return scaled.reshape(array_shape).astype(jnp.bfloat16)


def apply_experts(values, scale_rows, w_gate, w_up, w_down):
    inputs = dequantize(values, scale_rows)
    gate_part = jnp.einsum("pecd,edf->pecf", inputs, w_gate, preferred_element_type=jnp.float32)
    up_part = jnp.einsum("pecd,edf->pecf", inputs, w_up, preferred_element_type=jnp.float32)
    hidden = (jax.nn.silu(gate_part) * up_part).astype(jnp.bfloat16)
    return jnp.einsum("pecf,efd->pecd", hidden, w_down, preferred_element_type=jnp.float32).astype(
        jnp.bfloat16
    )


def routed(tokens, scales, expert_ids, gate_weights, w_gate, w_up, w_down):
    peer_count = lax.axis_size("expert")
    token_count, feature_width = tokens.shape
    top_count = expert_ids.shape[1]
    local_experts = w_gate.shape[0]
    expert_total = peer_count * local_experts
    capacity = 2 * token_count * top_count // expert_total
    blocks = scales.shape[1]
    flat_ids = expert_ids.reshape(-1)
    onehot = (flat_ids[:, None] == jnp.arange(expert_total, dtype=jnp.int32)[None, :]).astype(
        jnp.int32
    )
    position = jnp.sum((jnp.cumsum(onehot, axis=0) - onehot) * onehot, axis=1)
    slot_index = flat_ids * capacity + position
    source_token = jnp.arange(token_count * top_count, dtype=jnp.int32) // top_count
    send_values = (
        jnp.zeros((expert_total * capacity, feature_width), jnp.bfloat16)
        .at[slot_index]
        .set(tokens[source_token])
    )
    send_values = send_values.reshape(peer_count, local_experts, capacity, feature_width)
    send_scales = (
        jnp.zeros((expert_total * capacity, blocks), jnp.bfloat16)
        .at[slot_index]
        .set(scales[source_token])
    )
    send_scales = send_scales.reshape(peer_count, local_experts, capacity, blocks)
    outputs = apply_experts(
        lax.all_to_all(send_values, "expert", split_axis=0, concat_axis=0, tiled=True),
        lax.all_to_all(send_scales, "expert", split_axis=0, concat_axis=0, tiled=True),
        w_gate,
        w_up,
        w_down,
    )
    returned = lax.all_to_all(outputs, "expert", split_axis=0, concat_axis=0, tiled=True)
    gathered = returned.reshape(expert_total * capacity, feature_width)[slot_index]
    gathered = gathered.reshape(token_count, top_count, feature_width)
    combined = jnp.sum(gate_weights[:, :, None] * gathered.astype(jnp.float32), axis=1)
    return combined.astype(jnp.bfloat16)


def pack_kernel(expert_total, *refs):
    sources, out_ref, targets, sems = refs[:4], refs[4], refs[5:9], refs[9]
    tokens_ref, scales_ref, ids_ref, weights_ref = targets
    copies = [
        pltpu.make_async_copy(source, target, sems.at[index])
        for index, (source, target) in enumerate(zip(sources, targets, strict=True))
    ]
    for copy in copies:
        copy.start()
    count, width = tokens_ref.shape
    blocks = scales_ref.shape[0]
    size = width // blocks
    packed = out_ref.shape[1]
    square = (count, count)
    same = lax.broadcasted_iota(jnp.int32, square, 0) == lax.broadcasted_iota(jnp.int32, square, 1)
    same = same.astype(jnp.float32).astype(jnp.bfloat16)

    def turn(values):
        return lax.dot_general(
            same, values, (((1,), (1,)), ((), ())), preferred_element_type=jnp.float32
        )

    for copy in copies[1:]:
        copy.wait()
    line = lax.broadcasted_iota(jnp.int32, (packed - width, count), 0)
    dense = jnp.zeros(line.shape, jnp.float32)
    for k in range(ids_ref.shape[0]):
        dense += jnp.where(line % expert_total == ids_ref[k : k + 1, :], weights_ref[k : k + 1, :], 0.0)
    terms = jnp.zeros(line.shape, jnp.float32)
    for index in range(3):
        term = dense.astype(jnp.bfloat16).astype(jnp.float32)
        terms = jnp.where(line // expert_total == index, term, terms)
        dense = dense - term
    out_ref[:, width:] = turn(terms.astype(jnp.bfloat16)).astype(jnp.bfloat16)
    scales = turn(scales_ref[...])
    copies[0].wait()
    for block in range(blocks):
        columns = slice(block * size, (block + 1) * size)
        values = tokens_ref[:, columns].astype(jnp.float32) * scales[:, block : block + 1]
        out_ref[:, columns] = values.astype(jnp.bfloat16)


def pack_rows(tokens, scales, expert_ids, gate_weights, expert_total):
    count, width = tokens.shape
    packed = width + -(-3 * expert_total // LANES) * LANES
    arrays = (tokens, scales.T, expert_ids.T, gate_weights.T)
    return pl.pallas_call(
        functools.partial(pack_kernel, expert_total),
        in_specs=[pl.BlockSpec(memory_space=pl.ANY)] * 4,
        out_specs=pl.BlockSpec(memory_space=pltpu.VMEM),
        out_shape=jax.ShapeDtypeStruct((count, packed), jnp.bfloat16),
        scratch_shapes=[pltpu.VMEM(array.shape, array.dtype) for array in arrays]
        + [pltpu.SemaphoreType.DMA((4,))],
        compiler_params=pltpu.CompilerParams(vmem_limit_bytes=64 * 2**20),
        cost_estimate=pl.CostEstimate(flops=1, bytes_accessed=1, transcendentals=0),
    )(*arrays)


def experts_on(expert_total, me_ref, blocks, outs, gate_ref, up_ref, down_ref, hidden_ref):
    hidden_width, width = down_ref.shape[1:]
    inputs = jnp.concatenate([block[:, :width] for block in blocks], axis=0)
    for index in range(hidden_width // CHUNK):
        columns = slice(index * CHUNK, (index + 1) * CHUNK)
        gate_part = jnp.dot(inputs, gate_ref[0, :, columns], preferred_element_type=jnp.float32)
        up_part = jnp.dot(inputs, up_ref[0, :, columns], preferred_element_type=jnp.float32)
        hidden = gate_part / (1.0 + jnp.exp(-gate_part)) * up_part
        hidden_ref[:, columns] = hidden.astype(jnp.bfloat16)
    factors = []
    for block in blocks:
        terms = block[:, width:].astype(jnp.float32)
        lane = lax.broadcasted_iota(jnp.int32, terms.shape, 1) % expert_total
        factors.append(jnp.sum(jnp.where(lane == me_ref[0], terms, 0.0), axis=1, keepdims=True))
    factor = jnp.concatenate(factors, axis=0)
    hidden = hidden_ref[...]
    for start in range(0, width, 512):
        columns = slice(start, start + 512)
        result = jnp.dot(hidden, down_ref[0, :, columns], preferred_element_type=jnp.float32)
        result = factor * result.astype(jnp.bfloat16).astype(jnp.float32)
        row = 0
        for out in outs:
            out[:, columns] = result[row : row + out.shape[0], :].astype(out.dtype)
            row += out.shape[0]


def expert_kernel(expert_total, number, *refs):
    me_ref, blocks, weights, outs, hidden_ref = refs[0], refs[1 : 1 + number], refs[1 + number : 4 + number], refs[-4:-1], refs[-1]
    experts_on(expert_total, me_ref, blocks, outs, *weights, hidden_ref)


def first_kernel(expert_total, number, *refs):
    me_ref, blocks, sources, rest = refs[0], refs[1 : 1 + number], refs[1 + number : 4 + number], refs[4 + number :]
    outs, weights, hidden_ref, sems = rest[:3], rest[3:6], rest[6], rest[7]
    copies = []
    for index, (source, target) in enumerate(zip(sources, weights, strict=True)):
        half = source.shape[1] // 2
        for part in range(2):
            lines = slice(part * half, (part + 1) * half)
            copies.append(
                pltpu.make_async_copy(source.at[:, lines, :], target.at[:, lines, :], sems.at[2 * index + part])
            )
            copies[-1].start()
    for copy in copies:
        copy.wait()
    experts_on(expert_total, me_ref, blocks, outs, *weights, hidden_ref)


def weighted_outputs(expert_total, me, blocks, weights, first):
    count = blocks[0].shape[0]
    rows = sum(block.shape[0] for block in blocks)
    hidden_width, width = weights[2].shape[1:]
    vmem = pl.BlockSpec(memory_space=pltpu.VMEM)
    return pl.pallas_call(
        functools.partial(first_kernel if first else expert_kernel, expert_total, len(blocks)),
        in_specs=[pl.BlockSpec(memory_space=pltpu.SMEM)]
        + [vmem] * len(blocks)
        + [pl.BlockSpec(memory_space=pl.ANY) if first else vmem] * 3,
        out_specs=[vmem] * (6 if first else 3),
        out_shape=[
            jax.ShapeDtypeStruct((count, width), jnp.float32),
            jax.ShapeDtypeStruct((count, width), jnp.float32),
            jax.ShapeDtypeStruct((rows - 2 * count, width), jnp.bfloat16),
        ]
        + [jax.ShapeDtypeStruct(array.shape, array.dtype) for array in weights if first],
        scratch_shapes=[pltpu.VMEM((rows, hidden_width), jnp.bfloat16)]
        + [pltpu.SemaphoreType.DMA((6,))] * first,
        compiler_params=pltpu.CompilerParams(vmem_limit_bytes=FIRST_LIMIT if first else VMEM_LIMIT),
        cost_estimate=pl.CostEstimate(flops=1, bytes_accessed=1, transcendentals=0),
    )(me, *blocks, *weights)


def gathered(tokens, scales, expert_ids, gate_weights, w_gate, w_up, w_down):
    peer_count = lax.axis_size("expert")

    def exchange(array, mask):
        return lax.ppermute(array, "expert", [(i, i ^ mask) for i in range(peer_count)])

    def after(array, names):
        if not names:
            return array
        return lax.optimization_barrier((array,) + tuple(done[name] for name in names))[0]

    me = lax.axis_index("expert").astype(jnp.int32).reshape(1)
    weights = (w_gate, w_up, w_down)
    done = {"A0": pack_rows(tokens, scales, expert_ids, gate_weights, peer_count)}
    own, other, sums = {}, {}, {}
    for step, ties in STEPS:
        kind, number = step[0], int(step[1:] or 0)
        if kind == "W":
            one = after(jnp.ones((), jnp.bfloat16), ["A0"] + ties)
            weights = tuple(array * one for array in weights)
            done[step] = weights[-1]
        elif kind == "A":
            bit = number & -number if number % 4 else 1 << (number.bit_length() - 1)
            done[step] = exchange(after(done["A%d" % (number - bit)], ties), bit)
        elif kind == "B":
            pair = jnp.concatenate([done["A%d" % number], done["A%d" % (number + 2)]], axis=0)
            done[step] = exchange(after(pair, ties), 1)
        elif kind == "K":
            names = ["A%d" % number, "A%d" % (number + 2)]
            names += ["B%d" % number] if "B%d" % number in done else ["A%d" % (number + 1), "A%d" % (number + 3)]
            blocks = [done[name] for name in names]
            blocks[0] = after(blocks[0], ties)
            parts = weighted_outputs(peer_count, me, blocks, weights, step == FIRST)
            weights = parts[3:] or weights
            done[step] = parts[0]
            own[number], other[number] = parts[:2], parts[2]
        elif kind == "O":
            got = exchange(other[number], 1).astype(jnp.float32)
            count = got.shape[0] // 2
            done[step] = (own[number][1] + got[count:]).astype(jnp.bfloat16)
            own[number] = own[number][0] + got[:count]
        elif kind == "X":
            done[step] = exchange(after(done["O%d" % number], ties), 2)
            sums[number] = own[number] + done[step].astype(jnp.float32)
        elif kind == "Z":
            done[step] = exchange(after(sums[number].astype(jnp.bfloat16), ties), number)
    combined = sums[0]
    for z in range(4, peer_count, 4):
        combined = combined + done["Z%d" % z].astype(jnp.float32)
    return combined.astype(jnp.bfloat16)


def on_device(tokens, scales, expert_ids, gate_weights, w_gate, w_up, w_down):
    peer_count = lax.axis_size("expert")
    local_experts = w_gate.shape[0]
    capacity = 2 * tokens.shape[0] * expert_ids.shape[1] // (peer_count * local_experts)
    power_of_two = peer_count & (peer_count - 1) == 0
    whole = capacity >= tokens.shape[0] and local_experts == 1 and peer_count >= 4 and power_of_two
    layer = gathered if whole else routed
    return layer(tokens, scales, expert_ids, gate_weights, w_gate, w_up, w_down)


def solution(mesh):
    return jax.shard_map(
        on_device,
        mesh=mesh,
        in_specs=(
            P(("groups", "expert"), None),
            P(("groups", "expert"), None),
            P(("groups", "expert"), None),
            P(("groups", "expert"), None),
            P("expert", None, None),
            P("expert", None, None),
            P("expert", None, None),
        ),
        out_specs=P(("groups", "expert"), None),
        check_vma=False,
    )
```

```python
import functools

import jax
import jax.numpy as jnp
from jax import lax
from jax.experimental import pallas as pl
from jax.experimental.pallas import tpu as pltpu
from jax.sharding import PartitionSpec as P

LANES = 128
CHUNK = 256
FIRST = 'K0'
KERNEL_FLOPS = 1
FIRST_LIMIT = 41 * 2**20
STEPS = [
    ('A4', []),
    ('A8', []),
    ('A2', []),
    ('A1', []),
    ('A3', []),
    ('A12', []),
    ('A6', []),
    ('A5', []),
    ('A7', []),
    ('A10', ['A5']),
    ('A9', []),
    ('A11', []),
    ('A14', []),
    ('A13', []),
    ('A15', []),
    ('K0', []),
    ('K8', []),
    ('O8', []),
    ('X8', []),
    ('K4', []),
    ('O0', []),
    ('O4', []),
    ('X4', []),
    ('K12', ['O8']),
    ('O12', []),
    ('X12', []),
    ('X0', ['X12']),
    ('Z8', []),
    ('Z12', []),
    ('Z4', []),
]
VMEM_LIMIT = 24 * 2**20


def dequantize(values, scales):
    array_shape = values.shape
    blocks = scales.shape[-1]
    split_shape = array_shape[:-1] + (blocks, array_shape[-1] // blocks)
    scaled = values.astype(jnp.float32).reshape(split_shape) * scales.astype(jnp.float32)[..., None]
    return scaled.reshape(array_shape).astype(jnp.bfloat16)


def apply_experts(values, scale_rows, w_gate, w_up, w_down):
    inputs = dequantize(values, scale_rows)
    gate_part = jnp.einsum("pecd,edf->pecf", inputs, w_gate, preferred_element_type=jnp.float32)
    up_part = jnp.einsum("pecd,edf->pecf", inputs, w_up, preferred_element_type=jnp.float32)
    hidden = (jax.nn.silu(gate_part) * up_part).astype(jnp.bfloat16)
    return jnp.einsum("pecf,efd->pecd", hidden, w_down, preferred_element_type=jnp.float32).astype(
        jnp.bfloat16
    )


def routed(tokens, scales, expert_ids, gate_weights, w_gate, w_up, w_down):
    peer_count = lax.axis_size("expert")
    token_count, feature_width = tokens.shape
    top_count = expert_ids.shape[1]
    local_experts = w_gate.shape[0]
    expert_total = peer_count * local_experts
    capacity = 2 * token_count * top_count // expert_total
    blocks = scales.shape[1]
    flat_ids = expert_ids.reshape(-1)
    onehot = (flat_ids[:, None] == jnp.arange(expert_total, dtype=jnp.int32)[None, :]).astype(
        jnp.int32
    )
    position = jnp.sum((jnp.cumsum(onehot, axis=0) - onehot) * onehot, axis=1)
    slot_index = flat_ids * capacity + position
    source_token = jnp.arange(token_count * top_count, dtype=jnp.int32) // top_count
    send_values = (
        jnp.zeros((expert_total * capacity, feature_width), jnp.bfloat16)
        .at[slot_index]
        .set(tokens[source_token])
    )
    send_values = send_values.reshape(peer_count, local_experts, capacity, feature_width)
    send_scales = (
        jnp.zeros((expert_total * capacity, blocks), jnp.bfloat16)
        .at[slot_index]
        .set(scales[source_token])
    )
    send_scales = send_scales.reshape(peer_count, local_experts, capacity, blocks)
    outputs = apply_experts(
        lax.all_to_all(send_values, "expert", split_axis=0, concat_axis=0, tiled=True),
        lax.all_to_all(send_scales, "expert", split_axis=0, concat_axis=0, tiled=True),
        w_gate,
        w_up,
        w_down,
    )
    returned = lax.all_to_all(outputs, "expert", split_axis=0, concat_axis=0, tiled=True)
    gathered = returned.reshape(expert_total * capacity, feature_width)[slot_index]
    gathered = gathered.reshape(token_count, top_count, feature_width)
    combined = jnp.sum(gate_weights[:, :, None] * gathered.astype(jnp.float32), axis=1)
    return combined.astype(jnp.bfloat16)


def pack_kernel(expert_total, *refs):
    sources, out_ref, targets, sems = refs[:4], refs[4], refs[5:9], refs[9]
    tokens_ref, scales_ref, ids_ref, weights_ref = targets
    copies = [
        pltpu.make_async_copy(source, target, sems.at[index])
        for index, (source, target) in enumerate(zip(sources, targets, strict=True))
    ]
    for copy in copies:
        copy.start()
    count, width = tokens_ref.shape
    blocks = scales_ref.shape[0]
    size = width // blocks
    packed = out_ref.shape[1]
    square = (count, count)
    same = lax.broadcasted_iota(jnp.int32, square, 0) == lax.broadcasted_iota(jnp.int32, square, 1)
    same = same.astype(jnp.float32).astype(jnp.bfloat16)

    def turn(values):
        return lax.dot_general(
            same, values, (((1,), (1,)), ((), ())), preferred_element_type=jnp.float32
        )

    for copy in copies[1:]:
        copy.wait()
    line = lax.broadcasted_iota(jnp.int32, (packed - width, count), 0)
    dense = jnp.zeros(line.shape, jnp.float32)
    for k in range(ids_ref.shape[0]):
        dense += jnp.where(line % expert_total == ids_ref[k : k + 1, :], weights_ref[k : k + 1, :], 0.0)
    terms = jnp.zeros(line.shape, jnp.float32)
    for index in range(3):
        term = dense.astype(jnp.bfloat16).astype(jnp.float32)
        terms = jnp.where(line // expert_total == index, term, terms)
        dense = dense - term
    out_ref[:, width:] = turn(terms.astype(jnp.bfloat16)).astype(jnp.bfloat16)
    scales = turn(scales_ref[...])
    copies[0].wait()
    for block in range(blocks):
        columns = slice(block * size, (block + 1) * size)
        values = tokens_ref[:, columns].astype(jnp.float32) * scales[:, block : block + 1]
        out_ref[:, columns] = values.astype(jnp.bfloat16)


def pack_rows(tokens, scales, expert_ids, gate_weights, expert_total):
    count, width = tokens.shape
    packed = width + -(-3 * expert_total // LANES) * LANES
    arrays = (tokens, scales.T, expert_ids.T, gate_weights.T)
    return pl.pallas_call(
        functools.partial(pack_kernel, expert_total),
        in_specs=[pl.BlockSpec(memory_space=pl.ANY)] * 4,
        out_specs=pl.BlockSpec(memory_space=pltpu.VMEM),
        out_shape=jax.ShapeDtypeStruct((count, packed), jnp.bfloat16),
        scratch_shapes=[pltpu.VMEM(array.shape, array.dtype) for array in arrays]
        + [pltpu.SemaphoreType.DMA((4,))],
        compiler_params=pltpu.CompilerParams(vmem_limit_bytes=64 * 2**20),
        cost_estimate=pl.CostEstimate(flops=1, bytes_accessed=1, transcendentals=0),
    )(*arrays)


def experts_on(expert_total, me_ref, blocks, outs, gate_ref, up_ref, down_ref, hidden_ref):
    hidden_width, width = down_ref.shape[1:]
    inputs = jnp.concatenate([block[:, :width] for block in blocks], axis=0)
    for index in range(hidden_width // CHUNK):
        columns = slice(index * CHUNK, (index + 1) * CHUNK)
        gate_part = jnp.dot(inputs, gate_ref[0, :, columns], preferred_element_type=jnp.float32)
        up_part = jnp.dot(inputs, up_ref[0, :, columns], preferred_element_type=jnp.float32)
        hidden = gate_part / (1.0 + jnp.exp(-gate_part)) * up_part
        hidden_ref[:, columns] = hidden.astype(jnp.bfloat16)
    factors = []
    for block in blocks:
        terms = block[:, width:].astype(jnp.float32)
        lane = lax.broadcasted_iota(jnp.int32, terms.shape, 1) % expert_total
        factors.append(jnp.sum(jnp.where(lane == me_ref[0], terms, 0.0), axis=1, keepdims=True))
    factor = jnp.concatenate(factors, axis=0)
    hidden = hidden_ref[...]
    for start in range(0, width, 512):
        columns = slice(start, start + 512)
        result = jnp.dot(hidden, down_ref[0, :, columns], preferred_element_type=jnp.float32)
        result = factor * result.astype(jnp.bfloat16).astype(jnp.float32)
        row = 0
        for out in outs:
            out[:, columns] = result[row : row + out.shape[0], :].astype(out.dtype)
            row += out.shape[0]


def expert_kernel(expert_total, number, *refs):
    me_ref, blocks, weights, outs, hidden_ref = refs[0], refs[1 : 1 + number], refs[1 + number : 4 + number], refs[-4:-1], refs[-1]
    experts_on(expert_total, me_ref, blocks, outs, *weights, hidden_ref)


def first_kernel(expert_total, number, *refs):
    me_ref, blocks, sources, rest = refs[0], refs[1 : 1 + number], refs[1 + number : 4 + number], refs[4 + number :]
    outs, weights, hidden_ref, sems = rest[:3], rest[3:6], rest[6], rest[7]
    copies = []
    for index, (source, target) in enumerate(zip(sources, weights, strict=True)):
        half = source.shape[1] // 2
        for part in range(2):
            lines = slice(part * half, (part + 1) * half)
            copies.append(
                pltpu.make_async_copy(source.at[:, lines, :], target.at[:, lines, :], sems.at[2 * index + part])
            )
            copies[-1].start()
    for copy in copies:
        copy.wait()
    experts_on(expert_total, me_ref, blocks, outs, *weights, hidden_ref)


def weighted_outputs(expert_total, me, blocks, weights, first):
    count = blocks[0].shape[0]
    rows = sum(block.shape[0] for block in blocks)
    hidden_width, width = weights[2].shape[1:]
    vmem = pl.BlockSpec(memory_space=pltpu.VMEM)
    return pl.pallas_call(
        functools.partial(first_kernel if first else expert_kernel, expert_total, len(blocks)),
        in_specs=[pl.BlockSpec(memory_space=pltpu.SMEM)]
        + [vmem] * len(blocks)
        + [pl.BlockSpec(memory_space=pl.ANY) if first else vmem] * 3,
        out_specs=[vmem] * (6 if first else 3),
        out_shape=[
            jax.ShapeDtypeStruct((count, width), jnp.float32),
            jax.ShapeDtypeStruct((count, width), jnp.float32),
            jax.ShapeDtypeStruct((rows - 2 * count, width), jnp.bfloat16),
        ]
        + [jax.ShapeDtypeStruct(array.shape, array.dtype) for array in weights if first],
        scratch_shapes=[pltpu.VMEM((rows, hidden_width), jnp.bfloat16)]
        + [pltpu.SemaphoreType.DMA((6,))] * first,
        compiler_params=pltpu.CompilerParams(vmem_limit_bytes=FIRST_LIMIT if first else VMEM_LIMIT),
        cost_estimate=pl.CostEstimate(flops=KERNEL_FLOPS, bytes_accessed=1, transcendentals=0),
    )(me, *blocks, *weights)


def gathered(tokens, scales, expert_ids, gate_weights, w_gate, w_up, w_down):
    peer_count = lax.axis_size("expert")

    def exchange(array, mask):
        return lax.ppermute(array, "expert", [(i, i ^ mask) for i in range(peer_count)])

    def after(array, names):
        if not names:
            return array
        return lax.optimization_barrier((array,) + tuple(done[name] for name in names))[0]

    me = lax.axis_index("expert").astype(jnp.int32).reshape(1)
    weights = (w_gate, w_up, w_down)
    done = {"A0": pack_rows(tokens, scales, expert_ids, gate_weights, peer_count)}
    own, other, sums = {}, {}, {}
    for step, ties in STEPS:
        kind, number = step[0], int(step[1:] or 0)
        if kind == "W":
            one = after(jnp.ones((), jnp.bfloat16), ["A0"] + ties)
            weights = tuple(array * one for array in weights)
            done[step] = weights[-1]
        elif kind == "A":
            bit = number & -number
            done[step] = exchange(after(done["A%d" % (number - bit)], ties), bit)
        elif kind == "B":
            pair = jnp.concatenate([done["A%d" % number], done["A%d" % (number + 2)]], axis=0)
            done[step] = exchange(after(pair, ties), 1)
        elif kind == "K":
            names = ["A%d" % number, "A%d" % (number + 2)]
            names += ["B%d" % number] if "B%d" % number in done else ["A%d" % (number + 1), "A%d" % (number + 3)]
            blocks = [done[name] for name in names]
            blocks[0] = after(blocks[0], ties)
            parts = weighted_outputs(peer_count, me, blocks, weights, step == FIRST)
            weights = parts[3:] or weights
            done[step] = parts[0]
            own[number], other[number] = parts[:2], parts[2]
        elif kind == "O":
            got = exchange(after(other[number], ties), 1).astype(jnp.float32)
            count = got.shape[0] // 2
            done[step] = (own[number][1] + got[count:]).astype(jnp.bfloat16)
            own[number] = own[number][0] + got[:count]
        elif kind == "X":
            done[step] = exchange(after(done["O%d" % number], ties), 2)
            sums[number] = own[number] + done[step].astype(jnp.float32)
        elif kind == "Z":
            total = sums[number] + done["Z8"].astype(jnp.float32) if number == 12 else sums[number]
            done[step] = exchange(after(total.astype(jnp.bfloat16), ties), 12 if number == 12 else 4)
    combined = sums[0] + done["Z4"].astype(jnp.float32) + done["Z12"].astype(jnp.float32)
    return combined.astype(jnp.bfloat16)


def on_device(tokens, scales, expert_ids, gate_weights, w_gate, w_up, w_down):
    peer_count = lax.axis_size("expert")
    local_experts = w_gate.shape[0]
    capacity = 2 * tokens.shape[0] * expert_ids.shape[1] // (peer_count * local_experts)
    whole = capacity >= tokens.shape[0] and local_experts == 1 and peer_count == 16
    layer = gathered if whole else routed
    return layer(tokens, scales, expert_ids, gate_weights, w_gate, w_up, w_down)


def solution(mesh):
    return jax.shard_map(
        on_device,
        mesh=mesh,
        in_specs=(
            P(("groups", "expert"), None),
            P(("groups", "expert"), None),
            P(("groups", "expert"), None),
            P(("groups", "expert"), None),
            P("expert", None, None),
            P("expert", None, None),
            P("expert", None, None),
        ),
        out_specs=P(("groups", "expert"), None),
        check_vma=False,
    )
```
